32 devices in a mesh: dp: 2 (over y), mp: 16 (over z, x, core).
Axes of the slice: x: 2, y: 2, z: 4, core: 2. Of those that a mesh axis runs over, the one named last changes fastest.
Arguments:
- context: bfloat16 [128, 8192], P('dp', 'mp'), may hold values from -6 to 6
- attn_weight: bfloat16 [8192, 5120], P('mp', 'dp'), may hold values from -0.0625 to 0.0625
- stream: bfloat16 [128, 5120], P(('dp', 'mp')), may hold values from -6 to 6
- norm_gain: float32 [5120], replicated, may hold values from 0.1 to 1.9
- router_weight: bfloat16 [16, 5120], replicated, may hold values from -0.078125 to 0.078125
- expert_weights: bfloat16 [16, 3, 1536, 5120], P('mp', None, 'dp'), may hold values from -0.078125 to 0.078125
- inference_slot: int32 [16], replicated, may hold values from 0 to 15, each once
- routes: int32 [128, 6], P(('dp', 'mp')), may hold values from 0 to 15, all different within a row; in each aligned block of 4 rows (0 to 3, 4 to 7, ...) at most 2 rows name the same one
Outputs:
- hidden_out: bfloat16 [128, 5120], P(('dp', 'mp'))
- expert_mix: bfloat16 [128, 5120], P(('dp', 'mp'))
- placed_experts: bfloat16 [16, 3, 1536, 5120], P(None, None, ('dp', 'mp'))
The draws below stay inside these ranges and needn't reach their ends.
Inputs may be any that keep to these rules, and one draw needn't show every extreme that they name: inference_slot names each position once. `routes`: each row names 6 different experts. Within the rows of one device no expert is named by more than 2 rows, and in every draw some device names some expert exactly 2 times.
All inputs are finite; a program needn't handle non-finite values.
Results may differ from the reference program's by a relative error of at most 0.015.
Values may be sent and summed in bfloat16 or wider, within the bound.
A program may use at most 192 MiB of HBM per device.

```python
import math
import jax
import jax.numpy as jnp
import numpy as np
from jax import lax

D = 5120
FF = 1536
TOP = 6
ROWS_DEV = 4
EXPERTS = 16
CAP = 2
HV = 8192
ROWS = 128
N_DP = 2
N_MP = 16


def levels(own_key, dims, cuts, smallest, top_value):
    gain, own = 1.0, jax.random.fold_in(own_key, 6)
    for axis_at, blocks in cuts:
        draws = jnp.exp(jax.random.uniform(jax.random.fold_in(own, axis_at), (blocks,), jnp.float32, smallest / len(cuts), top_value / len(cuts)))
        gain = gain * jnp.repeat(draws, dims[axis_at] // blocks).reshape([-1 if axis == axis_at else 1 for axis in range(len(dims))])
    return gain


def shared_out(key, own, number, rows, number_of, top, reach, lean):
    ranking = jax.random.permutation(key, number_of)
    packed, ordinary = load_shares(number_of, rows * top, reach, lean, True), load_shares(number_of, rows * top, reach, lean, False)
    places = jnp.arange(number_of)

    def named(lengths, rotation):
        used = int((lengths > 0).sum())
        fixed = max(1, used // 4)
        shifted = fixed + (places - fixed + rotation * (used - fixed)) % max(1, number_of - fixed)
        return jnp.zeros((number_of,), jnp.int32).at[ranking[jnp.where(places < fixed, places, shifted)]].set(jnp.asarray(lengths, jnp.int32))

    lengths = jnp.where(number % 4 == 0, named(packed, number // 4), named(ordinary, number - number // 4 - 1))
    mixed = jax.random.permutation(jax.random.fold_in(own, 3), number_of)
    donor, sink = mixed[0:number_of // 2 * 2:2], mixed[1:number_of // 2 * 2:2]
    margin = jnp.minimum(lengths[donor] - 1, reach - lengths[sink]) // 2
    margin = jnp.where((donor == ranking[0]) | (sink == ranking[0]) | (lengths[sink] == 0), 0, jnp.maximum(margin, 0))
    shifted = jax.random.randint(jax.random.fold_in(own, 4), (number_of // 2,), 0, 1 << 20) % (margin + 1)
    lengths = lengths.at[donor].add(-shifted).at[sink].add(shifted)
    labels = jnp.searchsorted(jnp.cumsum(lengths), jnp.arange(rows * top), side="right").astype(jnp.int32)
    listing = labels.reshape(top, rows).T
    listing = listing[jax.random.permutation(jax.random.fold_in(own, 1), rows)]
    rotation = jax.random.randint(jax.random.fold_in(own, 2), (rows, 1), 0, top)
    return jnp.take_along_axis(listing, (jnp.arange(top)[None, :] + rotation) % top, axis=1)


def load_shares(number_of, total, bound, slope, full):
    weights = [(1 << 20) // math.isqrt(standing ** slope) + 1 for standing in range(1, number_of + 1)]
    largest = bound if full else min(bound, max(-(-total // number_of), total * weights[0] // sum(weights)))
    least = 1 if total - largest >= number_of - 1 else 0
    holding, surplus = [largest] + [least] * (number_of - 1), total - largest - least * (number_of - 1)
    while surplus > 0:
        free = [i for i in range(1, number_of) if holding[i] < largest] or [i for i in range(1, number_of) if holding[i] < bound]
        pool, left = sum([weights[i] for i in free]), surplus
        for i in free:
            more = min(bound - holding[i], max(1, left * weights[i] // pool), surplus)
            holding[i] = holding[i] + more
            surplus = surplus - more
    return np.array(holding)


def bell_draw(rng, extent, spread, reach, cuts=(), kind=jnp.bfloat16):
    gain = levels(rng, extent, cuts, -0.22, 0.18) if cuts else 1.0
    array = jax.random.normal(rng, extent, jnp.float32) * spread * gain
    return jnp.minimum(jnp.maximum(array, -reach), reach).astype(kind)


def setup_inputs(seed: int = 0) -> dict:
    key_list = jax.random.split(jax.random.key(seed), 9)
    context = bell_draw(key_list[0], (ROWS, HV), 1.0, 6.0, ((0, 2), (1, 16)))
    attn_weight = bell_draw(key_list[1], (HV, D), HV ** -0.5, 0.0625, ((0, 16), (1, 2)))
    stream = bell_draw(key_list[2], (ROWS, D), 1.0, 6.0, ((0, 32),))
    norm_gain = jnp.clip(1.0 + 0.18 * jax.random.normal(key_list[3], (D,), jnp.float32), 0.1, 1.9)
    router_weight = bell_draw(key_list[4], (EXPERTS, D), D ** -0.5, 0.078125)
    expert_weights = bell_draw(key_list[5], (EXPERTS, 3, FF, D), D ** -0.5, 0.078125, ((0, 16), (2, 2)))
    inference_slot = jax.random.permutation(key_list[6], EXPERTS).astype(jnp.int32)
    routes_keys = jax.random.split(jax.random.fold_in(key_list[7], 1), ROWS // ROWS_DEV)
    routes_turns = jax.random.permutation(jax.random.fold_in(key_list[7], 3), ROWS // ROWS_DEV)
    routes = jax.vmap(lambda own, number: shared_out(jax.random.fold_in(key_list[7], 2), own, number, ROWS_DEV, EXPERTS, TOP, CAP, 2))(routes_keys, routes_turns).reshape((ROWS, TOP))
    return {"context": context, "attn_weight": attn_weight, "stream": stream, "norm_gain": norm_gain, "router_weight": router_weight, "expert_weights": expert_weights, "inference_slot": inference_slot, "routes": routes}


def reference(context, attn_weight, stream, norm_gain, router_weight, expert_weights, inference_slot, routes):
    attended = jnp.dot(context, attn_weight, preferred_element_type=jnp.float32)
    hidden = (stream.astype(jnp.float32) + attended).astype(jnp.bfloat16)
    widened = hidden.astype(jnp.float32)
    normed = (widened * lax.rsqrt(lax.optimization_barrier(jnp.mean(widened * widened, axis=1, keepdims=True)) + 1e-06) * norm_gain).astype(jnp.bfloat16)
    scores = jax.nn.sigmoid(jnp.dot(normed, router_weight.T, preferred_element_type=jnp.float32))
    chosen = jnp.take_along_axis(scores, routes, axis=1)
    share = 2.5 * chosen / lax.optimization_barrier(jnp.sum(chosen, axis=1, keepdims=True))
    expert_ids = jnp.arange(EXPERTS, dtype=jnp.int32)
    source = lax.optimization_barrier(jnp.sum(jnp.where(inference_slot[:, None] == expert_ids[None, :], expert_ids[:, None], 0), axis=0)).astype(jnp.int32)
    placed = jnp.take(expert_weights, source, axis=0)
    flat_ids = routes.reshape(-1)
    slot_count = N_DP * N_MP * CAP
    row_index = (jnp.arange(flat_ids.shape[0], dtype=jnp.int32) // TOP).astype(jnp.int32)
    group_width = FF // N_DP

    def one_expert(running, expert):
        is_mine = flat_ids == expert
        position = (jnp.cumsum(is_mine.astype(jnp.int32)) - 1).astype(jnp.int32)
        target = jnp.where(is_mine, position, slot_count).astype(jnp.int32)
        picked = jnp.zeros((slot_count,), jnp.int32).at[target].set(row_index, mode='drop')
        row_data = normed[picked].astype(jnp.float32)
        expert_set = lax.dynamic_index_in_dim(placed, expert, 0, keepdims=False).astype(jnp.float32)
        gate_part = jnp.dot(row_data, expert_set[0].T, precision=lax.Precision.HIGHEST)
        up_part = jnp.dot(row_data, expert_set[1].T, precision=lax.Precision.HIGHEST)
        active = lax.optimization_barrier((jax.nn.silu(gate_part) * up_part).astype(jnp.bfloat16)).astype(jnp.float32)
        groups = active.reshape(slot_count, N_DP, group_width)
        down_part = expert_set[2].reshape(N_DP, group_width, D)
        partial_value = jnp.einsum('rjf,jfd->rjd', groups, down_part, precision=lax.Precision.HIGHEST)
        partial_value = lax.optimization_barrier(partial_value.astype(jnp.bfloat16)).astype(jnp.float32)
        answer = lax.optimization_barrier(jnp.sum(partial_value, axis=1)).astype(jnp.bfloat16)
        fetched = answer[jnp.clip(position, 0, slot_count - 1)].astype(jnp.float32)
        return (running + jnp.where(is_mine[:, None], fetched, jnp.float32(0.0)), None)
    start = jnp.zeros((flat_ids.shape[0], D), jnp.float32)
    gathered, unused = lax.scan(one_expert, start, expert_ids)
    per_choice = gathered.reshape(ROWS, TOP, D)
    expert_mix = lax.optimization_barrier(jnp.sum(share[:, :, None] * per_choice, axis=1)).astype(jnp.bfloat16)
    return (hidden, expert_mix, placed)
```

```python
import functools

import jax
import jax.numpy as jnp
from jax import lax
from jax.experimental import pallas as pl
from jax.experimental.pallas import tpu as pltpu
from jax.sharding import PartitionSpec as P

MESH = pl.DeviceIdType.MESH
PARTS = ((0, 1), (2,))


def offsets(count):
    half = count // 2
    order = [half]
    for step in range(1, half):
        order += [half - step, half + step]
    return [value for value in order if 0 < value < count]


def move_kernel(parts, first, *refs):
    weights, moved, send_sem, recv_sem, own_sem = refs if first else (refs[0],) + refs[2:]
    count = weights.shape[1]
    me, row = lax.axis_index("mp"), lax.axis_index("dp")
    barrier = pltpu.get_barrier_semaphore()
    for step in range(1, count):
        pl.semaphore_signal(
            barrier, inc=1, device_id=(row, lax.rem(me + step, count)), device_id_type=MESH
        )
    pl.semaphore_wait(barrier, count - 1)
    copies = []
    for step in offsets(count):
        peer = lax.rem(me + step, count)
        for at, part in enumerate(parts):
            copy = pltpu.make_async_remote_copy(
                src_ref=weights.at[part, peer],
                dst_ref=moved.at[me, part],
                send_sem=send_sem.at[at, step],
                recv_sem=recv_sem.at[at, step],
                device_id=(row, peer),
                device_id_type=MESH,
            )
            copy.start()
            copies.append(copy)
    own = []
    for at, part in enumerate(parts):
        copy = pltpu.make_async_copy(weights.at[part, me], moved.at[me, part], own_sem.at[at])
        copy.start()
        own.append(copy)
    for copy in own:
        copy.wait()
    for copy in copies:
        copy.wait_send()
    for copy in copies:
        copy.wait_recv()


def move(weights, held, parts, number):
    _, count, rows, width = weights.shape
    out = jax.ShapeDtypeStruct((count, 3, rows, width), weights.dtype)
    operands = (weights,) if held is None else (weights, held)
    size = len(parts) * count * rows * width * 2
    return pl.pallas_call(
        functools.partial(move_kernel, parts, held is None),
        out_shape=out,
        in_specs=[pl.BlockSpec(memory_space=pl.ANY)] * len(operands),
        out_specs=pl.BlockSpec(memory_space=pl.ANY),
        input_output_aliases={} if held is None else {1: 0},
        scratch_shapes=[
            pltpu.SemaphoreType.DMA((len(parts), count)),
            pltpu.SemaphoreType.DMA((len(parts), count)),
            pltpu.SemaphoreType.DMA((len(parts),)),
        ],
        compiler_params=pltpu.CompilerParams(collective_id=number, has_side_effects=True),
        cost_estimate=pl.CostEstimate(flops=0, bytes_accessed=size * 80, transcendentals=0),
    )(*operands)


def place_kernel(source_ref, moved_ref, out_ref):
    out_ref[...] = moved_ref[...]


def place(moved, source):
    count, three, rows, width = moved.shape
    return pl.pallas_call(
        place_kernel,
        out_shape=jax.ShapeDtypeStruct(moved.shape, moved.dtype),
        grid_spec=pltpu.PrefetchScalarGridSpec(
            num_scalar_prefetch=1,
            grid=(count,),
            in_specs=[
                pl.BlockSpec((1, three, rows, width), lambda i, source_ref: (source_ref[i], 0, 0, 0))
            ],
            out_specs=pl.BlockSpec((1, three, rows, width), lambda i, source_ref: (i, 0, 0, 0)),
        ),
        compiler_params=pltpu.CompilerParams(vmem_limit_bytes=24 * 2**20),
    )(source, moved)


def per_device(
    context, attn_weight, stream, norm_gain, router_weight, expert_weights, inference_slot, routes
):
    mp_count = lax.axis_size("mp")
    dp_count = lax.axis_size("dp")
    row_count, model_width = stream.shape
    me = lax.axis_index("mp")
    expert_ids = jnp.arange(mp_count, dtype=jnp.int32)
    named = inference_slot[:, None] == expert_ids[None, :]
    source = jnp.sum(jnp.where(named, expert_ids[:, None], 0), axis=0)
    hidden_units = expert_weights.shape[2]
    weights = expert_weights.reshape(3, mp_count, hidden_units // mp_count, model_width)
    column_width = attn_weight.shape[1]
    capacity = max(2, (7 * row_count * routes.shape[1] + 6 * mp_count - 1) // (6 * mp_count))

    whole_context = lax.all_gather(context, "dp", axis=0, tiled=True)
    partial_value = jnp.dot(whole_context, attn_weight, preferred_element_type=jnp.float32)
    partial_value = partial_value.astype(jnp.bfloat16).reshape(-1, row_count, column_width)
    spread = lax.all_to_all(partial_value, ("dp", "mp"), split_axis=0, concat_axis=0, tiled=True)
    attended = jnp.sum(
        spread.astype(jnp.float32).reshape(dp_count, mp_count, row_count, column_width), axis=1
    )
    attended = jnp.swapaxes(attended, 0, 1).reshape(row_count, model_width)
    hidden = (stream.astype(jnp.float32) + attended).astype(jnp.bfloat16)
    widened = hidden.astype(jnp.float32)
    normed = (
        widened * lax.rsqrt(jnp.mean(widened * widened, axis=1, keepdims=True) + 1e-06) * norm_gain
    ).astype(jnp.bfloat16)
    wide_ids = jnp.arange(-(-mp_count // 128) * 128, dtype=jnp.int32)
    naming = jnp.any(routes[:, :, None] == wide_ids[None, None, :], axis=1).astype(jnp.bfloat16)
    packet = jnp.concatenate([normed, naming], axis=1)
    packet, weights = lax.optimization_barrier((packet, weights))
    packets = lax.all_gather(packet, ("dp", "mp"), axis=0, tiled=True)
    moved = move(weights, None, PARTS[0], 0)
    packets, moved = lax.optimization_barrier((packets, moved))

    contract = (((1,), (1,)), ((), ()))
    mine = inference_slot[me] == expert_ids
    named_mine = jnp.any(
        (packets[:, model_width : model_width + mp_count] > 0) & mine[None, :], axis=1
    ).reshape(-1, row_count)
    picks = slot_picks(named_mine, capacity)
    groups = named_mine.shape[0]
    same = jnp.arange(groups)[:, None] == jnp.arange(groups)[None, :]
    picking = (same[:, None, :, None] & picks[:, :, None, :]).reshape(
        groups * capacity, groups * row_count
    )
    rows = jnp.dot(
        picking.astype(jnp.bfloat16),
        packets[:, :model_width],
        preferred_element_type=jnp.float32,
    ).astype(jnp.bfloat16)
    experts = expert_weights[0]
    gate = lax.dot_general(rows, experts[0], contract, preferred_element_type=jnp.float32)
    up = lax.dot_general(rows, experts[1], contract, preferred_element_type=jnp.float32)
    active = (jax.nn.silu(gate) * up).astype(jnp.bfloat16)
    answers = jnp.dot(active, experts[2], preferred_element_type=jnp.float32)
    answers = answers.astype(jnp.bfloat16).reshape(groups, capacity, model_width)
    returned = lax.all_to_all(answers, ("dp", "mp"), split_axis=0, concat_axis=0, tiled=True)
    returned, moved = lax.optimization_barrier((returned, moved))
    moved = move(weights, moved, PARTS[1], 1)

    logits = lax.dot_general(normed, router_weight, contract, preferred_element_type=jnp.float32)
    matches = naming[:, :mp_count] > 0
    chosen = jnp.where(matches, jax.nn.sigmoid(logits), 0.0)
    share = 2.5 * chosen / jnp.sum(chosen, axis=1, keepdims=True)
    by_holder = jnp.sum(
        jnp.where(named[:, None, :], share[None], 0.0), axis=2
    )
    holder_picks = slot_picks(
        jnp.any(named[:, None, :] & matches[None], axis=2), capacity
    )
    mixing = jnp.where(holder_picks, by_holder[:, None, :], 0.0).reshape(-1, row_count)
    results = jnp.sum(
        returned.astype(jnp.float32).reshape(dp_count, -1, model_width), axis=0
    )
    mix = jnp.dot(mixing.T, results, precision=lax.Precision.HIGHEST).astype(jnp.bfloat16)
    return (hidden, mix, place(moved, source))


def slot_picks(named, capacity):
    count = named.astype(jnp.int32)
    width = named.shape[1]
    before = jnp.arange(width)[:, None] < jnp.arange(width)[None, :]
    position = jnp.sum(jnp.where(before[None], count[:, :, None], 0), axis=1)
    return named[:, None, :] & (position[:, None, :] == jnp.arange(capacity)[None, :, None])


def solution(mesh):
    placed = (
        P("dp", "mp"),
        P("mp", "dp"),
        P(("dp", "mp"), None),
        P(),
        P(),
        P("mp", None, "dp", None),
        P(),
        P(("dp", "mp"), None),
    )
    return jax.shard_map(
        per_device,
        mesh=mesh,
        in_specs=placed,
        out_specs=(P(("dp", "mp"), None), P(("dp", "mp"), None), P(None, None, ("dp", "mp"), None)),
        check_vma=False,
    )
```

```python
import functools

import jax
import jax.numpy as jnp
from jax import lax
from jax.experimental import pallas as pl
from jax.experimental.pallas import tpu as pltpu
from jax.sharding import PartitionSpec as P

MESH = pl.DeviceIdType.MESH
PARTS = ((0, 1), (2,))


def offsets(count):
    half = count // 2
    order = [half]
    for step in range(1, half):
        order += [half - step, half + step]
    return [value for value in order if 0 < value < count]


def move_kernel(parts, ahead, weights, early, moved, send_sem, recv_sem, own_sem):
    count = weights.shape[1]
    half = count // 2
    me, row = lax.axis_index("mp"), lax.axis_index("dp")
    barrier = pltpu.get_barrier_semaphore()
    for step in range(1, count):
        pl.semaphore_signal(
            barrier, inc=1, device_id=(row, lax.rem(me + step, count)), device_id_type=MESH
        )
    pl.semaphore_wait(barrier, count - 1)
    copies = []
    for step in offsets(count):
        peer = lax.rem(me + step, count)
        for at, part in enumerate(parts):
            if part == ahead and step == half:
                continue
            copy = pltpu.make_async_remote_copy(
                src_ref=weights.at[part, peer],
                dst_ref=moved.at[me, at],
                send_sem=send_sem.at[at, step],
                recv_sem=recv_sem.at[at, step],
                device_id=(row, peer),
                device_id_type=MESH,
            )
            copy.start()
            copies.append(copy)
    own = []
    for at, part in enumerate(parts):
        own.append(pltpu.make_async_copy(weights.at[part, me], moved.at[me, at], own_sem.at[at]))
    own.append(
        pltpu.make_async_copy(
            early,
            moved.at[lax.rem(me + count - half, count), parts.index(ahead)],
            own_sem.at[len(parts)],
        )
    )
    for copy in own:
        copy.start()
    for copy in own:
        copy.wait()
    for copy in copies:
        copy.wait_send()
    for copy in copies:
        copy.wait_recv()


def move(weights, early, parts, number):
    _, count, rows, width = weights.shape
    size = len(parts) * count * rows * width * 2
    return pl.pallas_call(
        functools.partial(move_kernel, parts, parts[0]),
        out_shape=jax.ShapeDtypeStruct((count, len(parts), rows, width), weights.dtype),
        in_specs=[pl.BlockSpec(memory_space=pl.ANY)] * 2,
        out_specs=pl.BlockSpec(memory_space=pl.ANY),
        scratch_shapes=[
            pltpu.SemaphoreType.DMA((len(parts), count)),
            pltpu.SemaphoreType.DMA((len(parts), count)),
            pltpu.SemaphoreType.DMA((len(parts) + 1,)),
        ],
        compiler_params=pltpu.CompilerParams(collective_id=number, has_side_effects=True),
        cost_estimate=pl.CostEstimate(flops=0, bytes_accessed=size * 80, transcendentals=0),
    )(weights, early)


def cut_piece(weights, part):
    _, count, rows, width = weights.shape
    peer = lax.rem(lax.axis_index("mp") + count // 2, count)
    start = (jnp.int32(part), peer, jnp.int32(0), jnp.int32(0))
    return lax.dynamic_slice(weights, start, (1, 1, rows, width)).reshape(rows, width)


def send_ahead(piece):
    count = lax.axis_size("mp")
    half = count // 2
    return lax.ppermute(piece, "mp", [(i, (i + half) % count) for i in range(count)])


def place_kernel(*refs):
    moved_ref, out_ref = refs[1], refs[-1]
    out_ref[:, 0] = moved_ref[:, 0]


def place(moved, source, parts, held):
    count, number, rows, width = moved.shape
    first = parts[0]
    block = (1, 1, rows, width)
    operands = (source, moved) if held is None else (source, moved, held)
    in_specs = [pl.BlockSpec(block, lambda i, p, source_ref: (source_ref[i], p, 0, 0))]
    if held is not None:
        in_specs.append(pl.BlockSpec(memory_space=pl.ANY))
    return pl.pallas_call(
        place_kernel,
        out_shape=jax.ShapeDtypeStruct((count, 3, rows, width), moved.dtype),
        grid_spec=pltpu.PrefetchScalarGridSpec(
            num_scalar_prefetch=1,
            grid=(count, number),
            in_specs=in_specs,
            out_specs=pl.BlockSpec(block, lambda i, p, source_ref: (i, p + first, 0, 0)),
        ),
        input_output_aliases={} if held is None else {2: 0},
        compiler_params=pltpu.CompilerParams(vmem_limit_bytes=24 * 2**20),
        cost_estimate=pl.CostEstimate(
            flops=0, bytes_accessed=2 * moved.size * 2, transcendentals=0
        ),
    )(*operands)


def per_device(
    context, attn_weight, stream, norm_gain, router_weight, expert_weights, inference_slot, routes
):
    mp_count = lax.axis_size("mp")
    dp_count = lax.axis_size("dp")
    row_count, model_width = stream.shape
    me = lax.axis_index("mp")
    expert_ids = jnp.arange(mp_count, dtype=jnp.int32)
    named = inference_slot[:, None] == expert_ids[None, :]
    source = jnp.sum(jnp.where(named, expert_ids[:, None], 0), axis=0)
    hidden_units = expert_weights.shape[2]
    weights = expert_weights.reshape(3, mp_count, hidden_units // mp_count, model_width)
    column_width = attn_weight.shape[1]
    capacity = max(2, (7 * row_count * routes.shape[1] + 6 * mp_count - 1) // (6 * mp_count))

    first_piece, second_piece, context = lax.optimization_barrier(
        (cut_piece(weights, PARTS[0][0]), cut_piece(weights, PARTS[1][0]), context)
    )
    whole_context = lax.all_gather(context, "dp", axis=0, tiled=True)
    partial_value = jnp.dot(whole_context, attn_weight, preferred_element_type=jnp.float32)
    partial_value = partial_value.astype(jnp.bfloat16).reshape(-1, row_count, column_width)
    spread = lax.all_to_all(partial_value, ("dp", "mp"), split_axis=0, concat_axis=0, tiled=True)
    attended = jnp.sum(
        spread.astype(jnp.float32).reshape(dp_count, mp_count, row_count, column_width), axis=1
    )
    attended = jnp.swapaxes(attended, 0, 1).reshape(row_count, model_width)
    hidden = (stream.astype(jnp.float32) + attended).astype(jnp.bfloat16)
    widened = hidden.astype(jnp.float32)
    normed = (
        widened * lax.rsqrt(jnp.mean(widened * widened, axis=1, keepdims=True) + 1e-06) * norm_gain
    ).astype(jnp.bfloat16)
    wide_ids = jnp.arange(-(-mp_count // 128) * 128, dtype=jnp.int32)
    naming = jnp.any(routes[:, :, None] == wide_ids[None, None, :], axis=1).astype(jnp.bfloat16)
    packet = jnp.concatenate([normed, naming], axis=1)
    packet, early = lax.optimization_barrier((packet, send_ahead(first_piece)))
    packets = lax.all_gather(packet, ("dp", "mp"), axis=0, tiled=True)
    moved = move(weights, early, PARTS[0], 0)
    packets, moved, second_piece = lax.optimization_barrier((packets, moved, second_piece))
    early = send_ahead(second_piece)

    contract = (((1,), (1,)), ((), ()))
    mine = inference_slot[me] == expert_ids
    named_mine = jnp.any(
        (packets[:, model_width : model_width + mp_count] > 0) & mine[None, :], axis=1
    ).reshape(-1, row_count)
    picks = slot_picks(named_mine, capacity)
    groups = named_mine.shape[0]
    same = jnp.arange(groups)[:, None] == jnp.arange(groups)[None, :]
    picking = (same[:, None, :, None] & picks[:, :, None, :]).reshape(
        groups * capacity, groups * row_count
    )
    rows = jnp.dot(
        picking.astype(jnp.bfloat16),
        packets[:, :model_width],
        preferred_element_type=jnp.float32,
    ).astype(jnp.bfloat16)
    experts = expert_weights[0]
    gate = lax.dot_general(rows, experts[0], contract, preferred_element_type=jnp.float32)
    up = lax.dot_general(rows, experts[1], contract, preferred_element_type=jnp.float32)
    active = (jax.nn.silu(gate) * up).astype(jnp.bfloat16)
    answers = jnp.dot(active, experts[2], preferred_element_type=jnp.float32)
    answers = answers.astype(jnp.bfloat16).reshape(groups, capacity, model_width)
    answers, early = lax.optimization_barrier((answers, early))
    returned = lax.all_to_all(answers, ("dp", "mp"), split_axis=0, concat_axis=0, tiled=True)
    held = place(moved, source, PARTS[0], None)
    returned, held, early = lax.optimization_barrier((returned, held, early))
    moved = move(weights, early, PARTS[1], 1)

    logits = lax.dot_general(normed, router_weight, contract, preferred_element_type=jnp.float32)
    matches = naming[:, :mp_count] > 0
    chosen = jnp.where(matches, jax.nn.sigmoid(logits), 0.0)
    share = 2.5 * chosen / jnp.sum(chosen, axis=1, keepdims=True)
    by_holder = jnp.sum(
        jnp.where(named[:, None, :], share[None], 0.0), axis=2
    )
    holder_picks = slot_picks(
        jnp.any(named[:, None, :] & matches[None], axis=2), capacity
    )
    mixing = jnp.where(holder_picks, by_holder[:, None, :], 0.0).reshape(-1, row_count)
    results = jnp.sum(
        returned.astype(jnp.float32).reshape(dp_count, -1, model_width), axis=0
    )
    mix = jnp.dot(mixing.T, results, precision=lax.Precision.HIGHEST).astype(jnp.bfloat16)
    return (hidden, mix, place(moved, source, PARTS[1], held))


def slot_picks(named, capacity):
    count = named.astype(jnp.int32)
    width = named.shape[1]
    before = jnp.arange(width)[:, None] < jnp.arange(width)[None, :]
    position = jnp.sum(jnp.where(before[None], count[:, :, None], 0), axis=1)
    return named[:, None, :] & (position[:, None, :] == jnp.arange(capacity)[None, :, None])


def solution(mesh):
    placed = (
        P("dp", "mp"),
        P("mp", "dp"),
        P(("dp", "mp"), None),
        P(),
        P(),
        P("mp", None, "dp", None),
        P(),
        P(("dp", "mp"), None),
    )
    return jax.shard_map(
        per_device,
        mesh=mesh,
        in_specs=placed,
        out_specs=(P(("dp", "mp"), None), P(("dp", "mp"), None), P(None, None, ("dp", "mp"), None)),
        check_vma=False,
    )
```
